32 devices in a mesh: rep: 2 (over y), row: 4 (over z), col: 4 (over x, core).
Axes of the slice: x: 2, y: 2, z: 4, core: 2. Of those that a mesh axis runs over, the one named last changes fastest.
Arguments:
- grads: bfloat16 [2, 4096, 4096], P('rep', 'row', 'col'), may hold values from -4 to 4
- left_basis: float32 [4, 1024, 4096], P(None, 'rep', 'row'), may hold values from -0.09375 to 0.09375
- right_basis: float32 [4, 1024, 4096], P(None, 'rep', 'col'), may hold values from -0.09375 to 0.09375
- eigen_left: float32 [4096], P('row'), may hold values from 0.05 to 5
- eigen_right: float32 [4096], P('col'), may hold values from 0.05 to 5
Outputs:
- update: bfloat16 [4096, 4096], P('row', 'col')
The draws below stay inside these ranges and needn't reach their ends.
All inputs are finite; a program needn't handle non-finite values.
Results may differ from the reference program's by a relative error of at most 0.001.
Values may be sent and summed in bfloat16 or wider, within the bound.
A program may use at most 128 MiB of HBM per device.

```python
import math
import jax
import jax.numpy as jnp
from jax import lax

D = 4096
REPLICAS = 2
ROW_TILES = 4
COL_TILES = 4
TILE_R = 1024
TILE_C = 1024


def with_spikes(array, stream_key, source, target, blocks, factor):
    owner, partner = [(jnp.arange(array.shape[position]) // (array.shape[position] // blocks)).reshape([-1 if axis == position else 1 for axis in range(array.ndim)]) for position in (source, target)]
    chosen = jax.random.permutation(stream_key, blocks)[partner]
    strong = (owner == chosen) | (owner == (partner + blocks // 2) % blocks)
    return jnp.where(strong, factor * array, array)


def block_scale(stream_key, dims, shards, least, largest):
    def one(axis_at, blocks):
        steps = jax.random.uniform(jax.random.fold_in(jax.random.fold_in(stream_key, 6), axis_at), (blocks,), jnp.float32, least / len(shards), largest / len(shards))
        return jnp.repeat(jnp.exp(steps), dims[axis_at] // blocks).reshape((-1,) + (1,) * (len(dims) - axis_at - 1))

    loudness = one(*shards[0])
    for cut in shards[1:]:
        loudness = loudness * one(*cut)
    return loudness


def noise(own_key, extent, scale, limit, split=(), held_as=jnp.bfloat16):
    entries = jax.random.normal(own_key, extent, jnp.float32) * scale
    if len(split) > 0:
        entries = block_scale(own_key, extent, split, -0.22, 0.18) * entries
    return jnp.clip(entries, min=-limit, max=limit).astype(held_as)


def heavy_noise(rng, dims, width, limit, pieces, heavy, dtype=jnp.bfloat16):
    values = width * jax.random.normal(rng, dims, jnp.float32)
    if pieces:
        values = values * block_scale(rng, dims, pieces, -0.22, 0.18)
    return jnp.clip(with_spikes(values, jax.random.fold_in(rng, 3), *heavy), -limit, limit).astype(dtype)


def setup_inputs(seed: int = 0) -> dict:
    streams_of = jax.random.split(jax.random.key(seed), 6)
    return {
        "grads": heavy_noise(streams_of[0], (REPLICAS, D, D), 0.25, 4.0, ((0, 2), (1, 4), (2, 4)), (0, 1, 2, 2.0)),
        "left_basis": noise(streams_of[1], (ROW_TILES, TILE_R, D), D ** -0.5, 0.09375, ((1, 2), (2, 4)), jnp.float32),
        "right_basis": noise(streams_of[2], (COL_TILES, TILE_C, D), D ** -0.5, 0.09375, ((1, 2), (2, 4)), jnp.float32),
        "eigen_left": jnp.clip(jnp.exp(math.log(5.0) - 4.6051702 * jax.random.uniform(streams_of[3], (D,), jnp.float32) ** block_scale(streams_of[3], (D,), ((0, 4),), -0.2, 0.2)), 0.05, 5.0),
        "eigen_right": jnp.clip(jnp.exp(math.log(5.0) - 4.6051702 * jax.random.uniform(streams_of[4], (D,), jnp.float32) ** block_scale(streams_of[4], (D,), ((0, 4),), -0.2, 0.2)), 0.05, 5.0),
    }


epsilon = 1e-6


def reference(grads, left_basis, right_basis, eigen_left, eigen_right):
    highest = lax.Precision.HIGHEST

    def add_replica(index, total):
        piece = lax.dynamic_index_in_dim(grads, index, 0, keepdims=False)
        return total + piece.astype(jnp.float32)

    total = lax.fori_loop(0, REPLICAS, add_replica, jnp.zeros((D, D), jnp.float32))
    left = left_basis.reshape(D, D)
    right = right_basis.reshape(D, D)
    rotated_left = jnp.dot(left.T, total, precision=highest)
    rotated = jnp.dot(rotated_left, right, precision=highest)
    scaled = rotated / (eigen_left[:, None] + eigen_right[None, :] + epsilon)
    back = jnp.dot(scaled, right.T, precision=highest)
    update = jnp.dot(left, back, precision=highest)
    return update.astype(jnp.bfloat16)
```

```python
import jax
import jax.numpy as jnp
from jax import lax
from jax.sharding import PartitionSpec as P

epsilon = 1e-06


def body(grads, left_basis, right_basis, eigen_left, eigen_right):
    highest = lax.Precision.HIGHEST
    contract_first = (((0,), (0,)), ((), ()))
    contract_last = (((1,), (1,)), ((), ()))
    arrived = lax.all_to_all(grads, "rep", split_axis=1, concat_axis=0, tiled=True)
    summed = jnp.sum(arrived.astype(jnp.float32), axis=0)
    stacked = lax.all_gather(summed, "row", axis=0, tiled=True)
    left_piece = left_basis.reshape(-1, left_basis.shape[2])
    right_piece = right_basis.reshape(-1, right_basis.shape[2])
    left_done = lax.psum_scatter(
        lax.dot_general(stacked, left_piece, contract_first, precision=highest),
        "rep",
        scatter_dimension=0,
        tiled=True,
    )
    gathered = lax.all_gather(left_done, "col", axis=0, tiled=True)
    row_share = gathered.shape[1] // lax.axis_size("rep")
    block = gathered
    rotated = lax.psum_scatter(
        lax.dot_general(block, right_piece, contract_first, precision=highest),
        "rep",
        scatter_dimension=0,
        tiled=True,
    )
    offset = lax.axis_index("rep") * row_share
    left_eigen = lax.dynamic_slice_in_dim(eigen_left, offset, row_share)
    scaled_share = rotated / (left_eigen[:, None] + eigen_right[None, :] + epsilon)
    scaled = lax.all_gather(scaled_share, "rep", axis=0, tiled=True)
    block = right_piece
    back_share = lax.psum_scatter(
        lax.dot_general(block, scaled, contract_last, precision=highest),
        "col",
        scatter_dimension=0,
        tiled=True,
    )
    back_full = lax.all_gather(back_share, "rep", axis=0, tiled=True)
    block = left_piece
    out_share = lax.psum_scatter(
        lax.dot_general(block, back_full, contract_last, precision=highest),
        "row",
        scatter_dimension=0,
        tiled=True,
    ).astype(jnp.bfloat16)
    return lax.all_gather(out_share, "rep", axis=0, tiled=True)


CHUNKS_IN = 2
CHUNKS_MID = 2
CHUNKS_OUT = 2
GROUP = 128
SPAN = 240.0
LOW = -120.0
contract_first = (((0,), (0,)), ((), ()))
contract_last = (((1,), (1,)), ((), ()))


def matmul(a, b, dims):
    return lax.dot_general(
        a, b, dims, precision=lax.Precision.HIGH, preferred_element_type=jnp.float32
    )


def encode(x):
    rows, columns = x.shape
    groups = rows // GROUP
    top = jnp.max(jnp.abs(x).reshape(groups, GROUP, columns), axis=1)
    top = lax.reduce_precision(jnp.maximum(top, 1e-30) * 1.0078125, 8, 7)
    per_row = jnp.broadcast_to(
        (SPAN / top)[:, None, :], (groups, GROUP, columns)
    ).reshape(rows, columns)
    power = jnp.exp2(jnp.abs(x) * per_row + LOW)
    code = jnp.where(x < 0, -power, power).astype(jnp.bfloat16)
    scale = jnp.pad(top.astype(jnp.bfloat16), ((0, 16 - groups), (0, 0)))
    return jnp.concatenate([code, scale], axis=0)


def decode(coded):
    rows, columns = coded.shape[0] - 16, coded.shape[1]
    groups = rows // GROUP
    code = coded[:rows].astype(jnp.float32)
    top = coded[rows : rows + groups].astype(jnp.float32) * (1.0 / SPAN)
    per_row = jnp.broadcast_to(top[:, None, :], (groups, GROUP, columns)).reshape(
        rows, columns
    )
    size = (jnp.log2(jnp.abs(code)) - LOW) * per_row
    return jnp.where(code < 0, -size, size)


def shift(x, axis, step):
    n = lax.axis_size(axis)
    return lax.ppermute(x, axis, [(s, (s + step) % n) for s in range(n)])


def half(x, index, axis):
    size = x.shape[axis] // 2
    return lax.dynamic_slice_in_dim(x, index * size, size, axis)


def ordered(mine, peer, me, axis):
    return jnp.concatenate(
        [jnp.where(me == 0, mine, peer), jnp.where(me == 0, peer, mine)], axis=axis
    )


def scatter_blocks(blocks, axis, finish):
    n = lax.axis_size(axis)
    i = lax.axis_index(axis)
    sent = []
    for step in range(1, n):
        block = lax.dynamic_index_in_dim(blocks, lax.rem(i + step, n), 0, False)
        sent.append(shift(encode(block), axis, step))
    total = lax.dynamic_index_in_dim(blocks, i, 0, False)
    for got in sent:
        total = total + decode(got)
    return finish(total)


def pair_body(grads, left_basis, right_basis, eigen_left, eigen_right):
    me = lax.axis_index("rep")
    col = lax.axis_index("col")
    cols = lax.axis_size("col")
    blocks, tall, wide = left_basis.shape
    columns = right_basis.shape[2]

    grad = grads[0]
    keep, give = half(grad, me, 1), half(grad, 1 - me, 1)
    width = keep.shape[1] // CHUNKS_IN
    coded = []
    for c in range(CHUNKS_IN):
        at = slice(c * width, (c + 1) * width)
        got = shift(give[:, at], "rep", 1)
        coded.append(encode(keep[:, at].astype(jnp.float32) + got.astype(jnp.float32)))

    share = lax.dynamic_index_in_dim(left_basis, col, 0, False)
    share = shift(encode(share), "rep", 1)
    shares = [share] + [shift(share, "col", s) for s in range(1, cols)]
    rolled = jnp.stack([decode(s) for s in shares])
    place = lax.rem(col - jnp.arange(blocks) + cols, cols)
    other = jnp.take(rolled, place, axis=0, mode="clip")
    left = ordered(left_basis, other, me, 1).reshape(-1, wide)

    right = right_basis
    lines = right.shape[1]
    rotated = 0.0
    for c in range(CHUNKS_IN):
        stacked = lax.all_gather(coded[c], "row", axis=0)
        stacked = jnp.concatenate([decode(s) for s in stacked], axis=0)
        part = encode(matmul(stacked, left, contract_first))
        gathered = lax.all_gather(part, "col", axis=0)
        gathered = jnp.concatenate([decode(s) for s in gathered], axis=0)
        w = lines // CHUNKS_IN
        r = right[:, c * w : (c + 1) * w].reshape(-1, columns)
        rotated = rotated + matmul(gathered, r, contract_first)

    eigen = eigen_left[:, None] + eigen_right[None, :] + epsilon
    eigen = half(eigen, me, 0)
    keep, give = half(rotated, me, 0), half(rotated, 1 - me, 0)
    right_flat = right.reshape(-1, columns)
    high = keep.shape[0] // CHUNKS_MID
    backs = []
    for c in range(CHUNKS_MID):
        at = slice(c * high, (c + 1) * high)
        got = shift(encode(give[at]), "rep", 1)
        mine = (keep[at] + decode(got)) / eigen[at]
        peer = decode(shift(encode(mine), "rep", 1))
        scaled = ordered(mine, peer, me, 0)
        back = matmul(right_flat, scaled, contract_last)
        back = back.reshape(cols, -1, back.shape[1])
        backs.append(scatter_blocks(back, "col", lambda t: t))
    back = jnp.concatenate(
        [b[:, s * high : (s + 1) * high] for s in range(2) for b in backs], axis=1
    )

    narrow = back.shape[0] // CHUNKS_OUT
    mine, peer = [], []
    for c in range(CHUNKS_OUT):
        out = matmul(left, back[c * narrow : (c + 1) * narrow], contract_last)
        out = out.reshape(blocks, -1, narrow)
        done = scatter_blocks(out, "row", lambda t: t.astype(jnp.bfloat16))
        mine.append(done)
        peer.append(shift(done, "rep", 1))
    return ordered(
        jnp.concatenate(mine, axis=1), jnp.concatenate(peer, axis=1), me, 1
    )


def solution(mesh):
    placed = (
        P("rep", "row", "col"),
        P(None, "rep", "row"),
        P(None, "rep", "col"),
        P("row"),
        P("col"),
    )
    return jax.shard_map(
        pair_body if mesh.shape["rep"] == 2 else body,
        mesh=mesh,
        in_specs=placed,
        out_specs=P("row", "col"),
        check_vma=False,
    )
```

```python
import jax
import jax.numpy as jnp
from jax import lax
from jax.sharding import PartitionSpec as P

epsilon = 1e-06


def body(grads, left_basis, right_basis, eigen_left, eigen_right):
    highest = lax.Precision.HIGHEST
    contract_first = (((0,), (0,)), ((), ()))
    contract_last = (((1,), (1,)), ((), ()))
    arrived = lax.all_to_all(grads, "rep", split_axis=1, concat_axis=0, tiled=True)
    summed = jnp.sum(arrived.astype(jnp.float32), axis=0)
    stacked = lax.all_gather(summed, "row", axis=0, tiled=True)
    left_piece = left_basis.reshape(-1, left_basis.shape[2])
    right_piece = right_basis.reshape(-1, right_basis.shape[2])
    left_done = lax.psum_scatter(
        lax.dot_general(stacked, left_piece, contract_first, precision=highest),
        "rep",
        scatter_dimension=0,
        tiled=True,
    )
    gathered = lax.all_gather(left_done, "col", axis=0, tiled=True)
    row_share = gathered.shape[1] // lax.axis_size("rep")
    block = gathered
    rotated = lax.psum_scatter(
        lax.dot_general(block, right_piece, contract_first, precision=highest),
        "rep",
        scatter_dimension=0,
        tiled=True,
    )
    offset = lax.axis_index("rep") * row_share
    left_eigen = lax.dynamic_slice_in_dim(eigen_left, offset, row_share)
    scaled_share = rotated / (left_eigen[:, None] + eigen_right[None, :] + epsilon)
    scaled = lax.all_gather(scaled_share, "rep", axis=0, tiled=True)
    block = right_piece
    back_share = lax.psum_scatter(
        lax.dot_general(block, scaled, contract_last, precision=highest),
        "col",
        scatter_dimension=0,
        tiled=True,
    )
    back_full = lax.all_gather(back_share, "rep", axis=0, tiled=True)
    block = left_piece
    out_share = lax.psum_scatter(
        lax.dot_general(block, back_full, contract_last, precision=highest),
        "row",
        scatter_dimension=0,
        tiled=True,
    ).astype(jnp.bfloat16)
    return lax.all_gather(out_share, "rep", axis=0, tiled=True)


CHUNKS_IN = 2
CHUNKS_OUT = 2
GROUP = 128
SPAN = 240.0
LOW = -120.0
contract_first = (((0,), (0,)), ((), ()))
contract_last = (((1,), (1,)), ((), ()))


def matmul(a, b, dims):
    return lax.dot_general(
        a, b, dims, precision=lax.Precision.HIGH, preferred_element_type=jnp.float32
    )


def encode(x):
    rows, columns = x.shape
    groups = rows // GROUP
    top = jnp.max(jnp.abs(x).reshape(groups, GROUP, columns), axis=1)
    top = lax.reduce_precision(jnp.maximum(top, 1e-30) * 1.0078125, 8, 7)
    per_row = jnp.broadcast_to(
        (SPAN / top)[:, None, :], (groups, GROUP, columns)
    ).reshape(rows, columns)
    power = jnp.exp2(jnp.abs(x) * per_row + LOW)
    code = jnp.where(x < 0, -power, power).astype(jnp.bfloat16)
    scale = jnp.pad(top.astype(jnp.bfloat16), ((0, 16 - groups), (0, 0)))
    return jnp.concatenate([code, scale], axis=0)


def decode(coded):
    rows, columns = coded.shape[0] - 16, coded.shape[1]
    groups = rows // GROUP
    code = coded[:rows].astype(jnp.float32)
    top = coded[rows : rows + groups].astype(jnp.float32) * (1.0 / SPAN)
    per_row = jnp.broadcast_to(top[:, None, :], (groups, GROUP, columns)).reshape(
        rows, columns
    )
    size = (jnp.log2(jnp.abs(code)) - LOW) * per_row
    return jnp.where(code < 0, -size, size)


def shift(x, axis, step):
    n = lax.axis_size(axis)
    return lax.ppermute(x, axis, [(s, (s + step) % n) for s in range(n)])


def half(x, index, axis):
    size = x.shape[axis] // 2
    return lax.dynamic_slice_in_dim(x, index * size, size, axis)


def ordered(mine, peer, me, axis):
    return jnp.concatenate(
        [jnp.where(me == 0, mine, peer), jnp.where(me == 0, peer, mine)], axis=axis
    )


def after(later, earlier):
    later, earlier = lax.optimization_barrier((later, earlier))
    return later, earlier


def order_of(n):
    return sorted(range(1, n), key=lambda s: -min(s, n - s)) + [0]


def scatter_products(blocks, other, axis):
    n = lax.axis_size(axis)
    i = lax.axis_index(axis)
    sent, own = [], None
    for step in order_of(n):
        block = lax.dynamic_index_in_dim(blocks, lax.rem(i + step, n), 0, False)
        term = matmul(block, other, contract_last)
        if step == 0:
            own = term
        else:
            sent.append(shift(encode(term), axis, step))
    return own, sent


def add_up(own, sent):
    for got in sent:
        own = own + decode(got)
    return own


def pair_body(grads, left_basis, right_basis, eigen_left, eigen_right):
    me = lax.axis_index("rep")
    col = lax.axis_index("col")
    cols = lax.axis_size("col")
    blocks, tall, wide = left_basis.shape
    lines, columns = right_basis.shape[1:]

    grad = grads[0]
    keep, give = half(grad, me, 1), half(grad, 1 - me, 1)
    width = keep.shape[1] // CHUNKS_IN
    got = [
        shift(give[:, c * width : (c + 1) * width], "rep", 1) for c in range(CHUNKS_IN)
    ]
    coded = []
    for c in range(CHUNKS_IN):
        part, arrived = keep[:, c * width : (c + 1) * width], got[c]
        if c > 0:
            arrived, coded[c - 1] = after(arrived, coded[c - 1])
        coded.append(encode(part.astype(jnp.float32) + arrived.astype(jnp.float32)))

    share = shift(
        encode(lax.dynamic_index_in_dim(left_basis, col, 0, False)), "rep", 1
    )
    left = jnp.zeros((blocks, 2 * tall, wide), jnp.float32)
    left = lax.dynamic_update_slice(left, left_basis, (0, me * tall, 0))
    for step in range(cols):
        piece = share if step == 0 else shift(share, "col", step)
        place = lax.rem(col - step + cols, cols)
        left = lax.dynamic_update_slice(
            left, decode(piece)[None], (place, (1 - me) * tall, 0)
        )
    left_flat = left.reshape(-1, wide)

    keep = give = 0.0
    w = lines // CHUNKS_IN
    for c in range(CHUNKS_IN):
        stacked = lax.all_gather(coded[c], "row", axis=0)
        stacked = jnp.concatenate([decode(s) for s in stacked], axis=0)
        part = encode(matmul(stacked, left_flat, contract_first))
        gathered = lax.all_gather(part, "col", axis=0)
        r = right_basis[:, c * w : (c + 1) * w].reshape(-1, columns)
        for_peer = [decode(half(s, 1 - me, 1)) for s in gathered]
        give = give + matmul(jnp.concatenate(for_peer, axis=0), r, contract_first)
        for_me = [decode(half(s, me, 1)) for s in gathered]
        keep = keep + matmul(jnp.concatenate(for_me, axis=0), r, contract_first)

    eigen = eigen_left[:, None] + eigen_right[None, :] + epsilon
    mine = (keep + decode(shift(encode(give), "rep", 1))) / half(eigen, me, 0)
    peer = decode(shift(encode(mine), "rep", 1))
    first = scatter_products(right_basis, mine, "col")
    second = scatter_products(right_basis, peer, "col")
    back = ordered(add_up(*first), add_up(*second), me, 1)

    narrow = back.shape[0] // CHUNKS_OUT
    pending = [
        scatter_products(left, back[c * narrow : (c + 1) * narrow], "row")
        for c in range(CHUNKS_OUT)
    ]
    mine, peer = [], []
    for c, (own, sent) in enumerate(pending):
        if c > 0:
            own, mine[c - 1] = after(own, mine[c - 1])
        done = add_up(own, sent).astype(jnp.bfloat16)
        mine.append(done)
        peer.append(shift(done, "rep", 1))
    return ordered(
        jnp.concatenate(mine, axis=1), jnp.concatenate(peer, axis=1), me, 1
    )


def solution(mesh):
    placed = (
        P("rep", "row", "col"),
        P(None, "rep", "row"),
        P(None, "rep", "col"),
        P("row"),
        P("col"),
    )
    return jax.shard_map(
        pair_body if mesh.shape["rep"] == 2 else body,
        mesh=mesh,
        in_specs=placed,
        out_specs=P("row", "col"),
        check_vma=False,
    )
```

```python
import functools
import jax
import jax.numpy as jnp
from jax import lax
from jax.experimental import pallas as pl
from jax.experimental.pallas import tpu as pltpu
from jax.sharding import PartitionSpec as P

epsilon = 1e-06


def body(grads, left_basis, right_basis, eigen_left, eigen_right):
    highest = lax.Precision.HIGHEST
    contract_first = (((0,), (0,)), ((), ()))
    contract_last = (((1,), (1,)), ((), ()))
    arrived = lax.all_to_all(grads, "rep", split_axis=1, concat_axis=0, tiled=True)
    summed = jnp.sum(arrived.astype(jnp.float32), axis=0)
    stacked = lax.all_gather(summed, "row", axis=0, tiled=True)
    left_piece = left_basis.reshape(-1, left_basis.shape[2])
    right_piece = right_basis.reshape(-1, right_basis.shape[2])
    left_done = lax.psum_scatter(
        lax.dot_general(stacked, left_piece, contract_first, precision=highest),
        "rep",
        scatter_dimension=0,
        tiled=True,
    )
    gathered = lax.all_gather(left_done, "col", axis=0, tiled=True)
    row_share = gathered.shape[1] // lax.axis_size("rep")
    block = gathered
    rotated = lax.psum_scatter(
        lax.dot_general(block, right_piece, contract_first, precision=highest),
        "rep",
        scatter_dimension=0,
        tiled=True,
    )
    offset = lax.axis_index("rep") * row_share
    left_eigen = lax.dynamic_slice_in_dim(eigen_left, offset, row_share)
    scaled_share = rotated / (left_eigen[:, None] + eigen_right[None, :] + epsilon)
    scaled = lax.all_gather(scaled_share, "rep", axis=0, tiled=True)
    block = right_piece
    back_share = lax.psum_scatter(
        lax.dot_general(block, scaled, contract_last, precision=highest),
        "col",
        scatter_dimension=0,
        tiled=True,
    )
    back_full = lax.all_gather(back_share, "rep", axis=0, tiled=True)
    block = left_piece
    out_share = lax.psum_scatter(
        lax.dot_general(block, back_full, contract_last, precision=highest),
        "row",
        scatter_dimension=0,
        tiled=True,
    ).astype(jnp.bfloat16)
    return lax.all_gather(out_share, "rep", axis=0, tiled=True)


CHUNKS_IN = 2
CHUNKS_OUT = 2
GROUP = 128
SPAN = 240.0
LOW = -120.0
contract_first = (((0,), (0,)), ((), ()))
contract_last = (((1,), (1,)), ((), ()))


def matmul(a, b, dims):
    return lax.dot_general(
        a, b, dims, precision=lax.Precision.HIGH, preferred_element_type=jnp.float32
    )


def encode(x):
    rows, columns = x.shape
    groups = rows // GROUP
    top = jnp.max(jnp.abs(x).reshape(groups, GROUP, columns), axis=1)
    top = lax.reduce_precision(jnp.maximum(top, 1e-30) * 1.0078125, 8, 7)
    per_row = jnp.broadcast_to(
        (SPAN / top)[:, None, :], (groups, GROUP, columns)
    ).reshape(rows, columns)
    power = jnp.exp2(jnp.abs(x) * per_row + LOW)
    code = jnp.where(x < 0, -power, power).astype(jnp.bfloat16)
    scale = jnp.pad(top.astype(jnp.bfloat16), ((0, 16 - groups), (0, 0)))
    return jnp.concatenate([code, scale], axis=0)


def decode(coded):
    rows, columns = coded.shape[0] - 16, coded.shape[1]
    groups = rows // GROUP
    code = coded[:rows].astype(jnp.float32)
    top = coded[rows : rows + groups].astype(jnp.float32) * (1.0 / SPAN)
    per_row = jnp.broadcast_to(top[:, None, :], (groups, GROUP, columns)).reshape(
        rows, columns
    )
    size = (jnp.log2(jnp.abs(code)) - LOW) * per_row
    return jnp.where(code < 0, -size, size)


def shift(x, axis, step):
    n = lax.axis_size(axis)
    return lax.ppermute(x, axis, [(s, (s + step) % n) for s in range(n)])


def half(x, index, axis):
    size = x.shape[axis] // 2
    return lax.dynamic_slice_in_dim(x, index * size, size, axis)


def ordered(mine, peer, me, axis):
    return jnp.concatenate(
        [jnp.where(me == 0, mine, peer), jnp.where(me == 0, peer, mine)], axis=axis
    )


def after(later, earlier):
    later, earlier = lax.optimization_barrier((later, earlier))
    return later, earlier


def order_of(n):
    return sorted(range(1, n), key=lambda s: -min(s, n - s)) + [0]


def split(x):
    high = x.astype(jnp.bfloat16)
    return high, (x - high.astype(jnp.float32)).astype(jnp.bfloat16)


def product_kernel(coded, index_ref, a_ref, b_ref, out_ref, a_high, a_low):
    @pl.when(pl.program_id(0) == 0)
    def _():
        a_high[...], a_low[...] = split(a_ref[0])

    b_high, b_low = split(b_ref[...])
    dot = functools.partial(
        lax.dot_general,
        dimension_numbers=contract_last,
        preferred_element_type=jnp.float32,
    )
    high, low = a_high[...], a_low[...]
    term = dot(high, b_high) + (dot(high, b_low) + dot(low, b_high))
    if not coded:
        out_ref[...] = term
        return
    rows, columns = term.shape
    tops = []
    for g in range(rows // GROUP):
        at = slice(g * GROUP, (g + 1) * GROUP)
        x = term[at]
        size = jnp.abs(x)
        top = jnp.max(size, axis=0, keepdims=True)
        top = (jnp.maximum(top, 1e-30) * 1.0078125).astype(jnp.bfloat16)
        top = top.astype(jnp.float32)
        power = jnp.exp2(size * (SPAN / top) + LOW)
        out_ref[at, :] = jnp.where(x < 0, -power, power).astype(jnp.bfloat16)
        tops.append(top)
    tops.append(jnp.zeros((16 - len(tops), columns), jnp.float32))
    out_ref[rows:, :] = jnp.concatenate(tops, axis=0).astype(jnp.bfloat16)


def product(blocks, index, other, coded):
    rows, depth = blocks.shape[1:]
    columns = other.shape[0]
    tile = min(256, columns)
    out_rows = rows + 16 if coded else rows
    return pl.pallas_call(
        functools.partial(product_kernel, coded),
        out_shape=jax.ShapeDtypeStruct(
            (out_rows, columns), jnp.bfloat16 if coded else jnp.float32
        ),
        grid_spec=pltpu.PrefetchScalarGridSpec(
            num_scalar_prefetch=1,
            grid=(columns // tile,),
            in_specs=[
                pl.BlockSpec((1, rows, depth), lambda n, index: (index[0], 0, 0)),
                pl.BlockSpec((tile, depth), lambda n, index: (n, 0)),
            ],
            out_specs=pl.BlockSpec((out_rows, tile), lambda n, index: (0, n)),
            scratch_shapes=[pltpu.VMEM((rows, depth), jnp.bfloat16)] * 2,
        ),
        compiler_params=pltpu.CompilerParams(vmem_limit_bytes=40 * 2**20),
        cost_estimate=pl.CostEstimate(
            flops=6 * rows * depth * columns,
            bytes_accessed=4 * (rows + columns) * depth + 2 * rows * columns,
            transcendentals=0,
        ),
    )(index.astype(jnp.int32).reshape(1), blocks, other)


def scatter_products(blocks, other, axis):
    n = lax.axis_size(axis)
    i = lax.axis_index(axis)
    sent, own = [], None
    for step in order_of(n):
        index = lax.rem(i + step, n)
        if step == 0:
            own = product(blocks, index, other, False)
        else:
            sent.append(shift(product(blocks, index, other, True), axis, step))
    return own, sent


def add_up(own, sent):
    for got in sent:
        own = own + decode(got)
    return own


def pair_body(grads, left_basis, right_basis, eigen_left, eigen_right):
    me = lax.axis_index("rep")
    col = lax.axis_index("col")
    cols = lax.axis_size("col")
    blocks, tall, wide = left_basis.shape
    lines, columns = right_basis.shape[1:]

    grad = grads[0]
    keep, give = half(grad, me, 1), half(grad, 1 - me, 1)
    width = keep.shape[1] // CHUNKS_IN
    got = [
        shift(give[:, c * width : (c + 1) * width], "rep", 1) for c in range(CHUNKS_IN)
    ]
    coded = []
    for c in range(CHUNKS_IN):
        part, arrived = keep[:, c * width : (c + 1) * width], got[c]
        if c > 0:
            arrived, coded[c - 1] = after(arrived, coded[c - 1])
        coded.append(encode(part.astype(jnp.float32) + arrived.astype(jnp.float32)))

    share = shift(
        encode(lax.dynamic_index_in_dim(left_basis, col, 0, False)), "rep", 1
    )
    left = jnp.zeros((blocks, 2 * tall, wide), jnp.float32)
    left = lax.dynamic_update_slice(left, left_basis, (0, me * tall, 0))
    for step in range(cols):
        piece = share if step == 0 else shift(share, "col", step)
        place = lax.rem(col - step + cols, cols)
        left = lax.dynamic_update_slice(
            left, decode(piece)[None], (place, (1 - me) * tall, 0)
        )
    left_flat = left.reshape(-1, wide)

    keep = give = 0.0
    w = lines // CHUNKS_IN
    for c in range(CHUNKS_IN):
        stacked = lax.all_gather(coded[c], "row", axis=0)
        stacked = jnp.concatenate([decode(s) for s in stacked], axis=0)
        part = encode(matmul(stacked, left_flat, contract_first))
        gathered = lax.all_gather(part, "col", axis=0)
        r = right_basis[:, c * w : (c + 1) * w].reshape(-1, columns)
        for_peer = [decode(half(s, 1 - me, 1)) for s in gathered]
        give = give + matmul(jnp.concatenate(for_peer, axis=0), r, contract_first)
        for_me = [decode(half(s, me, 1)) for s in gathered]
        keep = keep + matmul(jnp.concatenate(for_me, axis=0), r, contract_first)

    eigen = eigen_left[:, None] + eigen_right[None, :] + epsilon
    mine = (keep + decode(shift(encode(give), "rep", 1))) / half(eigen, me, 0)
    peer = decode(shift(encode(mine), "rep", 1))
    first = scatter_products(right_basis, mine, "col")
    second = scatter_products(right_basis, peer, "col")
    back = ordered(add_up(*first), add_up(*second), me, 1)

    narrow = back.shape[0] // CHUNKS_OUT
    pending = [
        scatter_products(left, back[c * narrow : (c + 1) * narrow], "row")
        for c in range(CHUNKS_OUT)
    ]
    mine, peer = [], []
    for c, (own, sent) in enumerate(pending):
        if c > 0:
            own, mine[c - 1] = after(own, mine[c - 1])
        done = add_up(own, sent).astype(jnp.bfloat16)
        mine.append(done)
        peer.append(shift(done, "rep", 1))
    return ordered(
        jnp.concatenate(mine, axis=1), jnp.concatenate(peer, axis=1), me, 1
    )


def solution(mesh):
    placed = (
        P("rep", "row", "col"),
        P(None, "rep", "row"),
        P(None, "rep", "col"),
        P("row"),
        P("col"),
    )
    return jax.shard_map(
        pair_body if mesh.shape["rep"] == 2 else body,
        mesh=mesh,
        in_specs=placed,
        out_specs=P("row", "col"),
        check_vma=False,
    )
```

```python
import functools
import jax
import jax.numpy as jnp
from jax import lax
from jax.experimental import pallas as pl
from jax.experimental.pallas import tpu as pltpu
from jax.sharding import PartitionSpec as P

epsilon = 1e-06


def body(grads, left_basis, right_basis, eigen_left, eigen_right):
    highest = lax.Precision.HIGHEST
    contract_first = (((0,), (0,)), ((), ()))
    contract_last = (((1,), (1,)), ((), ()))
    arrived = lax.all_to_all(grads, "rep", split_axis=1, concat_axis=0, tiled=True)
    summed = jnp.sum(arrived.astype(jnp.float32), axis=0)
    stacked = lax.all_gather(summed, "row", axis=0, tiled=True)
    left_piece = left_basis.reshape(-1, left_basis.shape[2])
    right_piece = right_basis.reshape(-1, right_basis.shape[2])
    left_done = lax.psum_scatter(
        lax.dot_general(stacked, left_piece, contract_first, precision=highest),
        "rep",
        scatter_dimension=0,
        tiled=True,
    )
    gathered = lax.all_gather(left_done, "col", axis=0, tiled=True)
    row_share = gathered.shape[1] // lax.axis_size("rep")
    block = gathered
    rotated = lax.psum_scatter(
        lax.dot_general(block, right_piece, contract_first, precision=highest),
        "rep",
        scatter_dimension=0,
        tiled=True,
    )
    offset = lax.axis_index("rep") * row_share
    left_eigen = lax.dynamic_slice_in_dim(eigen_left, offset, row_share)
    scaled_share = rotated / (left_eigen[:, None] + eigen_right[None, :] + epsilon)
    scaled = lax.all_gather(scaled_share, "rep", axis=0, tiled=True)
    block = right_piece
    back_share = lax.psum_scatter(
        lax.dot_general(block, scaled, contract_last, precision=highest),
        "col",
        scatter_dimension=0,
        tiled=True,
    )
    back_full = lax.all_gather(back_share, "rep", axis=0, tiled=True)
    block = left_piece
    out_share = lax.psum_scatter(
        lax.dot_general(block, back_full, contract_last, precision=highest),
        "row",
        scatter_dimension=0,
        tiled=True,
    ).astype(jnp.bfloat16)
    return lax.all_gather(out_share, "rep", axis=0, tiled=True)


CHUNKS_IN = 2
CHUNKS_OUT = 2
GROUP = 128
SPAN = 240.0
LOW = -120.0
contract_first = (((0,), (0,)), ((), ()))
contract_last = (((1,), (1,)), ((), ()))


def matmul(a, b, dims):
    return lax.dot_general(
        a, b, dims, precision=lax.Precision.HIGH, preferred_element_type=jnp.float32
    )


def encode(x):
    rows, columns = x.shape
    groups = rows // GROUP
    top = jnp.max(jnp.abs(x).reshape(groups, GROUP, columns), axis=1)
    top = lax.reduce_precision(jnp.maximum(top, 1e-30) * 1.0078125, 8, 7)
    per_row = jnp.broadcast_to(
        (SPAN / top)[:, None, :], (groups, GROUP, columns)
    ).reshape(rows, columns)
    power = jnp.exp2(jnp.abs(x) * per_row + LOW)
    code = jnp.where(x < 0, -power, power).astype(jnp.bfloat16)
    scale = jnp.pad(top.astype(jnp.bfloat16), ((0, 16 - groups), (0, 0)))
    return jnp.concatenate([code, scale], axis=0)


def decode(coded):
    rows, columns = coded.shape[0] - 16, coded.shape[1]
    groups = rows // GROUP
    code = coded[:rows].astype(jnp.float32)
    top = coded[rows : rows + groups].astype(jnp.float32) * (1.0 / SPAN)
    per_row = jnp.broadcast_to(top[:, None, :], (groups, GROUP, columns)).reshape(
        rows, columns
    )
    size = (jnp.log2(jnp.abs(code)) - LOW) * per_row
    return jnp.where(code < 0, -size, size)


def shift(x, axis, step):
    n = lax.axis_size(axis)
    return lax.ppermute(x, axis, [(s, (s + step) % n) for s in range(n)])


def half(x, index, axis):
    size = x.shape[axis] // 2
    return lax.dynamic_slice_in_dim(x, index * size, size, axis)


def ordered(mine, peer, me, axis):
    return jnp.concatenate(
        [jnp.where(me == 0, mine, peer), jnp.where(me == 0, peer, mine)], axis=axis
    )


def after(later, earlier):
    later, earlier = lax.optimization_barrier((later, earlier))
    return later, earlier


def order_of(n):
    return sorted(range(1, n), key=lambda s: -min(s, n - s)) + [0]


def split(x):
    high = x.astype(jnp.bfloat16)
    return high, (x - high.astype(jnp.float32)).astype(jnp.bfloat16)


def product_kernel(coded, index_ref, a_ref, b_ref, out_ref, a_high, a_low):
    @pl.when(pl.program_id(0) == 0)
    def _():
        a_high[...], a_low[...] = split(a_ref[0])

    b_high, b_low = split(b_ref[...])
    dot = functools.partial(
        lax.dot_general,
        dimension_numbers=contract_last,
        preferred_element_type=jnp.float32,
    )
    high, low = a_high[...], a_low[...]
    term = dot(high, b_high) + (dot(high, b_low) + dot(low, b_high))
    if not coded:
        out_ref[...] = term
        return
    rows, columns = term.shape
    tops = []
    for g in range(rows // GROUP):
        at = slice(g * GROUP, (g + 1) * GROUP)
        x = term[at]
        size = jnp.abs(x)
        top = jnp.max(size, axis=0, keepdims=True)
        top = (jnp.maximum(top, 1e-30) * 1.0078125).astype(jnp.bfloat16)
        top = top.astype(jnp.float32)
        power = jnp.exp2(size * (SPAN / top) + LOW)
        out_ref[at, :] = jnp.where(x < 0, -power, power).astype(jnp.bfloat16)
        tops.append(top)
    tops.append(jnp.zeros((16 - len(tops), columns), jnp.float32))
    out_ref[rows:, :] = jnp.concatenate(tops, axis=0).astype(jnp.bfloat16)


def product(blocks, index, other, coded):
    rows, depth = blocks.shape[1:]
    columns = other.shape[0]
    tile = min(256, columns)
    out_rows = rows + 16 if coded else rows
    return pl.pallas_call(
        functools.partial(product_kernel, coded),
        out_shape=jax.ShapeDtypeStruct(
            (out_rows, columns), jnp.bfloat16 if coded else jnp.float32
        ),
        grid_spec=pltpu.PrefetchScalarGridSpec(
            num_scalar_prefetch=1,
            grid=(columns // tile,),
            in_specs=[
                pl.BlockSpec((1, rows, depth), lambda n, index: (index[0], 0, 0)),
                pl.BlockSpec((tile, depth), lambda n, index: (n, 0)),
            ],
            out_specs=pl.BlockSpec((out_rows, tile), lambda n, index: (0, n)),
            scratch_shapes=[pltpu.VMEM((rows, depth), jnp.bfloat16)] * 2,
        ),
        compiler_params=pltpu.CompilerParams(vmem_limit_bytes=40 * 2**20),
        cost_estimate=pl.CostEstimate(
            flops=6 * rows * depth * columns,
            bytes_accessed=4 * (rows + columns) * depth + 2 * rows * columns,
            transcendentals=0,
        ),
    )(index.astype(jnp.int32).reshape(1), blocks, other)


def scatter_products(blocks, other, axis):
    n = lax.axis_size(axis)
    i = lax.axis_index(axis)
    sent, own = [], None
    for step in order_of(n):
        index = lax.rem(i + step, n)
        if step == 0:
            own = product(blocks, index, other, False)
        else:
            sent.append(shift(product(blocks, index, other, True), axis, step))
    return own, sent


def add_up(own, sent):
    for got in sent:
        own = own + decode(got)
    return own


def pair_body(grads, left_basis, right_basis, eigen_left, eigen_right):
    me = lax.axis_index("rep")
    col = lax.axis_index("col")
    cols = lax.axis_size("col")
    blocks, tall, wide = left_basis.shape
    lines, columns = right_basis.shape[1:]

    grad = grads[0]
    keep, give = half(grad, me, 1), half(grad, 1 - me, 1)
    width = keep.shape[1] // CHUNKS_IN
    got = [
        shift(give[:, c * width : (c + 1) * width], "rep", 1) for c in range(CHUNKS_IN)
    ]
    coded = []
    for c in range(CHUNKS_IN):
        part, arrived = keep[:, c * width : (c + 1) * width], got[c]
        if c > 0:
            arrived, coded[c - 1] = after(arrived, coded[c - 1])
        coded.append(encode(part.astype(jnp.float32) + arrived.astype(jnp.float32)))

    share = shift(
        encode(lax.dynamic_index_in_dim(left_basis, col, 0, False)), "rep", 1
    )
    left = jnp.zeros((blocks, 2 * tall, wide), jnp.float32)
    left = lax.dynamic_update_slice(left, left_basis, (0, me * tall, 0))
    for step in range(cols):
        piece = share if step == 0 else shift(share, "col", step)
        place = lax.rem(col - step + cols, cols)
        left = lax.dynamic_update_slice(
            left, decode(piece)[None], (place, (1 - me) * tall, 0)
        )
    left_flat = left.reshape(-1, wide)

    keep = give = 0.0
    w = lines // CHUNKS_IN
    for c in range(CHUNKS_IN):
        stacked = lax.all_gather(coded[c], "row", axis=0)
        stacked = jnp.concatenate([decode(s) for s in stacked], axis=0)
        part = encode(matmul(stacked, left_flat, contract_first))
        gathered = [part] + [shift(part, "col", step) for step in range(1, cols)]
        r = jnp.concatenate(
            [
                lax.dynamic_slice(
                    right_basis,
                    (lax.rem(col - step + cols, cols), c * w, 0),
                    (1, w, columns),
                )[0]
                for step in range(cols)
            ],
            axis=0,
        )
        for_peer = [decode(half(s, 1 - me, 1)) for s in gathered]
        give = give + matmul(jnp.concatenate(for_peer, axis=0), r, contract_first)
        for_me = [decode(half(s, me, 1)) for s in gathered]
        keep = keep + matmul(jnp.concatenate(for_me, axis=0), r, contract_first)

    eigen = eigen_left[:, None] + eigen_right[None, :] + epsilon
    mine = (keep + decode(shift(encode(give), "rep", 1))) / half(eigen, me, 0)
    peer = decode(shift(encode(mine), "rep", 1))
    first = scatter_products(right_basis, mine, "col")
    second = scatter_products(right_basis, peer, "col")
    back = ordered(add_up(*first), add_up(*second), me, 1)

    narrow = back.shape[0] // CHUNKS_OUT
    pending = [
        scatter_products(left, back[c * narrow : (c + 1) * narrow], "row")
        for c in range(CHUNKS_OUT)
    ]
    mine, peer = [], []
    for c, (own, sent) in enumerate(pending):
        if c > 0:
            own, mine[c - 1] = after(own, mine[c - 1])
        done = add_up(own, sent).astype(jnp.bfloat16)
        mine.append(done)
        peer.append(shift(done, "rep", 1))
    return ordered(
        jnp.concatenate(mine, axis=1), jnp.concatenate(peer, axis=1), me, 1
    )


def solution(mesh):
    placed = (
        P("rep", "row", "col"),
        P(None, "rep", "row"),
        P(None, "rep", "col"),
        P("row"),
        P("col"),
    )
    return jax.shard_map(
        pair_body if mesh.shape["rep"] == 2 else body,
        mesh=mesh,
        in_specs=placed,
        out_specs=P("row", "col"),
        check_vma=False,
    )
```
